256 devices in a mesh: replica: 4 (over z_lo, core), vocab: 64 (over x, y, z_hi).
Axes of the slice: x: 4, y: 4, z: 8 (z_hi: 4, z_lo: 2; z = z_hi * 2 + z_lo), core: 2. Of those that a mesh axis runs over, the one named last changes fastest.
Arguments:
- codes: bfloat16 [4, 8192, 16384], P('replica', None, 'vocab'), may hold values from -1 to 1
- block_scales: bfloat16 [4, 64, 16384], P('replica', None, 'vocab'), may hold values from 0.0055236816 to 0.05517578
- outer_head: bfloat16 [8192, 16384], P('replica', 'vocab'), may hold values from -0.1875 to 0.1875
- momentum: float32 [8192, 16384], P('replica', 'vocab'), may hold values from -0.06629126 to 0.06629126
- hidden: bfloat16 [4, 1536, 8192], P('replica', 'vocab'), may hold values from -204 to 204
- targets: int32 [4, 1536], P('replica'), may hold values from 0 to 16383
Outputs:
- loss: float32 [4, 1536], P('replica', 'vocab')
The draws below stay inside these ranges and needn't reach their ends.
All inputs are finite; a program needn't handle non-finite values.
Results may differ from the reference program's by a relative error of at most 0.0011.
Values may be sent and summed in bfloat16 or wider, within the bound.
No kernel may reach another device: no remote copies, remote signals or barrier semaphores. Data moves between devices by JAX's collectives and lax.ppermute only.
A program may use at most 128 MiB of HBM per device.

```python
import math
import jax
import jax.numpy as jnp
from jax import lax

H = 8192
BLOCK = 128
REPLICAS = 4
V = 16384
TOK = 1536


def draw_hidden(key, part):
    key = jax.random.fold_in(key, 7)
    first = jax.random.fold_in(key, 0)
    return jax.random.truncated_normal(first, -6.0, 6.0, (REPLICAS, TOK, H), jnp.float32).astype(jnp.bfloat16)


def set_ends(result, stream_key, least, largest):
    shape = result.shape
    spot = [jax.random.randint(jax.random.fold_in(stream_key, axis), (), 0, shape[axis]) for axis in range(len(shape))]
    result = result.at[tuple(spot)].set(least)
    longest = shape.index(max(shape))
    spot[longest] = (spot[longest] + 1) % shape[longest]
    return result.at[tuple(spot)].set(largest)


def block_scale(rng, dims, cuts, low, largest):
    gain = 1.0
    for dim, blocks in cuts:
        draws = jax.random.uniform(jax.random.fold_in(jax.random.fold_in(rng, 6), dim), (blocks,), jnp.float32, low / len(cuts), largest / len(cuts))
        gain = gain * jnp.repeat(jnp.exp(draws), dims[dim] // blocks).reshape((-1,) + (1,) * (len(dims) - 1 - dim))
    return gain


def normal_values(rng, dims, width, most, pieces=(), dtype=jnp.bfloat16):
    level = block_scale(rng, dims, pieces, -0.22, 0.18) if pieces else 1.0
    result = jax.random.normal(rng, dims, jnp.float32) * width * level
    return jnp.minimum(jnp.maximum(result, -most), most).astype(dtype)


def setup_inputs(seed: int = 0) -> dict:
    key_of = jax.random.split(jax.random.key(seed), 7)
    codes = jnp.clip(jax.random.uniform(key_of[0], (REPLICAS, H, V), jnp.float32, -1.0, 1.0) * block_scale(key_of[0], (REPLICAS, H, V), ((0, 4), (2, 64)), -0.4, 0.0), -1.0, 1.0).astype(jnp.bfloat16)
    block_scales = jnp.clip(jnp.exp(math.log(0.05517578) - 2.3014795 * jax.random.uniform(key_of[1], (REPLICAS, H // BLOCK, V), jnp.float32) ** block_scale(key_of[1], (REPLICAS, H // BLOCK, V), ((0, 4), (2, 64)), -0.2, 0.2)), 0.0055236816, 0.05517578).astype(jnp.bfloat16)
    outer_head = normal_values(key_of[2], (H, V), (H // 9) ** -0.5, 0.1875, ((0, 4), (1, 64)))
    momentum = normal_values(key_of[3], (H, V), (1.0 / H ** 0.5), 0.06629126, ((0, 4), (1, 64)), jnp.float32)
    hidden = draw_hidden(jax.random.fold_in(key_of[6], 71), 0)
    targets = set_ends(jax.random.randint(key_of[5], (REPLICAS, TOK), 0, V), jax.random.fold_in(key_of[5], 1), 0, V - 1).astype(jnp.int32)
    return {"codes": codes, "block_scales": block_scales, "outer_head": outer_head, "momentum": momentum, "hidden": hidden, "targets": targets}


outer_mu = 0.9
outer_lr = 0.7


def reference(codes, block_scales, outer_head, momentum, hidden, targets):
    def add_one(total, pair):
        code, scale = pair
        term = code.astype(jnp.float32).reshape(H // BLOCK, BLOCK, V) * scale.astype(jnp.float32)[:, None, :]
        return total + term.reshape(H, V), None

    total, _ = lax.scan(add_one, jnp.zeros((H, V), jnp.float32), (codes, block_scales))
    pseudo = total * (1.0 / REPLICAS)
    velocity = outer_mu * momentum + pseudo
    new_head = (outer_head.astype(jnp.float32) - outer_lr * (pseudo + outer_mu * velocity)).astype(jnp.bfloat16)

    def one_replica(pair):
        rows, wanted = pair
        logits = jnp.dot(rows, new_head, preferred_element_type=jnp.float32)
        top = jnp.max(logits, axis=1)
        totals = jnp.sum(jnp.exp(logits - top[:, None]), axis=1)
        picked = jnp.take_along_axis(logits, wanted[:, None].astype(jnp.int32), axis=1)[:, 0]
        return top + jnp.log(totals) - picked

    return lax.map(one_replica, (hidden, targets))
```

```python
import jax
import jax.numpy as jnp
from jax import lax
from jax.sharding import Mesh, PartitionSpec as P

outer_mu = 0.9
outer_lr = 0.7

REP = ("zlo", "core")
VOC = ("x", "y", "zhi")
SWAP = [(0, 1), (1, 0)]


def shards(codes, block_scales, outer_head, momentum, hidden, targets):
    zlo = lax.axis_index("zlo")
    core = lax.axis_index("core")
    replicas = 4
    rows, width = outer_head.shape
    tok = hidden.shape[1]
    f32, bf16 = jnp.float32, jnp.bfloat16

    hid = hidden[0].reshape(tok, replicas, rows).transpose(1, 0, 2)
    hid = lax.all_to_all(hid, REP, 0, 0, tiled=True)
    hid = lax.all_gather(hid, ("y", "zhi"), axis=0, tiled=False)
    groups = hid.shape[0]
    lhs = hid.reshape(groups * replicas * tok, rows)

    blocks = block_scales.shape[1] // replicas
    per = rows // blocks
    c4 = codes.reshape(2, 2, rows, width)
    s4 = block_scales.reshape(2, 2, blocks, width)
    mine_c = lax.dynamic_index_in_dim(c4, core, 1, False)
    mine_s = lax.dynamic_index_in_dim(s4, core, 1, False)
    got_c = lax.ppermute(lax.dynamic_index_in_dim(c4, 1 - core, 1, False), "core", SWAP)
    got_s = lax.ppermute(lax.dynamic_index_in_dim(s4, 1 - core, 1, False), "core", SWAP)

    def chip_sum(z):
        def term(c, s):
            c = lax.dynamic_index_in_dim(c, z, 0, False).astype(f32)
            s = lax.dynamic_index_in_dim(s, z, 0, False).astype(f32)
            return c.reshape(blocks, per, width) * s[:, None, :]
        return (term(mine_c, mine_s) + term(got_c, got_s)).reshape(rows, width)

    other = lax.ppermute(chip_sum(1 - zlo).astype(bf16), "zlo", SWAP)
    pseudo = (chip_sum(zlo) + other.astype(f32)) * (1.0 / replicas)
    velocity = outer_mu * momentum + pseudo
    new_rows = (outer_head.astype(f32) - outer_lr * (pseudo + outer_mu * velocity)).astype(bf16)

    rhs = lax.all_gather(new_rows, "x", axis=0, tiled=False)
    nx = rhs.shape[0]
    rhs = rhs.transpose(1, 0, 2).reshape(rows, nx * width)
    part = jnp.dot(lhs, rhs, preferred_element_type=f32)

    part = part.reshape(groups, 2, 2, tok, nx * width)
    half = lax.ppermute(lax.dynamic_index_in_dim(part, 1 - core, 2, False), "core", SWAP)
    half = half + lax.dynamic_index_in_dim(part, core, 2, False)
    rest = lax.ppermute(lax.dynamic_index_in_dim(half, 1 - zlo, 1, False), "zlo", SWAP)
    logits = (rest + lax.dynamic_index_in_dim(half, zlo, 1, False)).reshape(groups * tok, nx * width)

    yz = lax.axis_index(("y", "zhi"))
    x = lax.axis_index("x")
    ids = (lax.broadcasted_iota(jnp.int32, (nx, width), 0) * groups + yz) * width
    ids = (ids + lax.broadcasted_iota(jnp.int32, (nx, width), 1)).reshape(1, nx * width)
    want = lax.dynamic_slice_in_dim(targets[0], x * groups * tok, groups * tok, 0)
    top = jnp.max(logits, axis=1)
    total = jnp.sum(jnp.exp(logits - top[:, None]), axis=1)
    picked = jnp.sum(jnp.where(ids == want[:, None], logits, 0.0), axis=1)
    stats = jnp.stack([a.reshape(groups, tok) for a in (top, total, picked)], axis=1)
    stats = lax.all_to_all(stats, ("y", "zhi"), 0, 0, tiled=True)
    top, total, picked = stats[:, 0], stats[:, 1], stats[:, 2]
    high = jnp.max(top, axis=0)
    total = jnp.sum(total * jnp.exp(top - high), axis=0)
    loss = high + jnp.log(total) - jnp.sum(picked, axis=0)
    return loss[None, :]


def solution(mesh):
    fine = Mesh(mesh.devices.reshape(2, 2, 4, 4, 4), REP + VOC)
    placed = (
        P(REP, None, VOC),
        P(REP, None, VOC),
        P(REP, VOC),
        P(REP, VOC),
        P(REP, VOC, None),
        P(REP, None),
    )
    return jax.shard_map(shards, mesh=fine, in_specs=placed, out_specs=P(REP, VOC), check_vma=False)
```

```python
import jax
import jax.numpy as jnp
from jax import lax
from jax.sharding import Mesh, PartitionSpec as P

outer_mu = 0.9
outer_lr = 0.7

REP = ("zlo", "core")
VOC = ("x", "y", "zhi")
SWAP = [(0, 1), (1, 0)]
PARTS = 2


def pick(a, i, axis):
    return lax.dynamic_index_in_dim(a, i, axis, False)


def shift(a, axis, by):
    n = lax.axis_size(axis)
    return lax.ppermute(a, axis, [(i, (i + by) % n) for i in range(n)])


def ring(a, axis):
    half = a.shape[0] // 2
    lower = shift(a, axis, 1)
    upper = shift(a, axis, -1)
    far0 = shift(lower[:half], axis, 1)
    far1 = shift(upper[half:], axis, -1)
    return lower, upper, far0, far1


def shards(codes, block_scales, outer_head, momentum, hidden, targets):
    zlo = lax.axis_index("zlo")
    core = lax.axis_index("core")
    x = lax.axis_index("x")
    y = lax.axis_index("y")
    zhi = lax.axis_index("zhi")
    replicas = 4
    rows, width = outer_head.shape
    tok = hidden.shape[1]
    f32, bf16 = jnp.float32, jnp.bfloat16

    hid = hidden[0].reshape(tok, replicas, rows).transpose(1, 0, 2)
    hid = lax.all_to_all(hid, REP, 0, 0, tiled=True)

    blocks = block_scales.shape[1] // replicas
    per = rows // blocks
    c4 = codes.reshape(2, 2, rows, width)
    s4 = block_scales.reshape(2, 2, blocks, width)
    mine_s = pick(s4, core, 1)
    got_s = lax.ppermute(pick(s4, 1 - core, 1), "core", SWAP)
    mine_c = pick(c4, core, 1)
    sent_c = pick(c4, 1 - core, 1)
    pr, pb = rows // PARTS, blocks // PARTS
    news = []
    for p in range(PARTS):
        mc = mine_c[:, p * pr:(p + 1) * pr]
        gc = lax.ppermute(sent_c[:, p * pr:(p + 1) * pr], "core", SWAP)
        ms = mine_s[:, p * pb:(p + 1) * pb]
        gs = got_s[:, p * pb:(p + 1) * pb]

        def chip_sum(z):
            def term(c, s):
                return pick(c, z, 0).astype(f32).reshape(pb, per, width) * pick(s, z, 0).astype(f32)[:, None, :]
            return (term(mc, ms) + term(gc, gs)).reshape(pr, width)

        other = lax.ppermute(chip_sum(1 - zlo).astype(bf16), "zlo", SWAP)
        pseudo = (chip_sum(zlo) + other.astype(f32)) * (1.0 / replicas)
        velocity = outer_mu * momentum[p * pr:(p + 1) * pr] + pseudo
        old = outer_head[p * pr:(p + 1) * pr].astype(f32)
        news.append((old - outer_lr * (pseudo + outer_mu * velocity)).astype(bf16))

    half = replicas // 2
    lhs = jnp.zeros((4, 4, replicas, tok, rows), bf16)

    def put(buf, a, dy, dz, r0):
        return lax.dynamic_update_slice(buf, a[None, None], ((y + dy) % 4, (zhi + dz) % 4, r0, 0, 0))

    lo, up, f0, f1 = ring(hid, "zhi")
    for dz, blk in ((0, hid), (-1, lo), (1, up), (2, jnp.concatenate([f0, f1], 0))):
        l1, u1, g0, g1 = ring(blk, "y")
        lhs = put(lhs, blk, 0, dz, 0)
        lhs = put(lhs, l1, -1, dz, 0)
        lhs = put(lhs, u1, 1, dz, 0)
        lhs = put(lhs, g0, 2, dz, 0)
        lhs = put(lhs, g1, 2, dz, half)
    groups = 16
    lhs = lhs.reshape(groups * replicas * tok, rows)

    rings = [ring(n, "x") for n in news]
    chunks = [
        (0, jnp.concatenate(news, 0)),
        (-1, jnp.concatenate([r[0] for r in rings], 0)),
        (1, jnp.concatenate([r[1] for r in rings], 0)),
        (2, jnp.concatenate([f for r in rings for f in r[2:]], 0)),
    ]

    yz = y * 4 + zhi
    want = lax.dynamic_slice_in_dim(targets[0], x * groups * tok, groups * tok, 0)
    stats = []
    for dx, rhs in chunks:
        part = jnp.dot(lhs, rhs, preferred_element_type=f32)
        part = part.reshape(groups, 2, 2, tok, width)
        both = lax.ppermute(pick(part, 1 - core, 2), "core", SWAP) + pick(part, core, 2)
        rest = lax.ppermute(pick(both, 1 - zlo, 1), "zlo", SWAP)
        logits = (rest + pick(both, zlo, 1)).reshape(groups * tok, width)
        first = (((x + dx) % 4) * groups + yz) * width
        ids = lax.broadcasted_iota(jnp.int32, (1, width), 1) + first
        top = jnp.max(logits, axis=1)
        stats.append(top)
        stats.append(jnp.sum(jnp.exp(logits - top[:, None]), axis=1))
        stats.append(jnp.sum(jnp.where(ids == want[:, None], logits, 0.0), axis=1))
    stats = jnp.stack([a.reshape(groups, tok) for a in stats], axis=1)
    stats = lax.all_to_all(stats, ("y", "zhi"), 0, 0, tiled=True)
    stats = stats.reshape(groups * len(chunks), 3, tok)
    top, total, picked = stats[:, 0], stats[:, 1], stats[:, 2]
    high = jnp.max(top, axis=0)
    total = jnp.sum(total * jnp.exp(top - high), axis=0)
    loss = high + jnp.log(total) - jnp.sum(picked, axis=0)
    return loss[None, :]


def solution(mesh):
    fine = Mesh(mesh.devices.reshape(2, 2, 4, 4, 4), REP + VOC)
    placed = (
        P(REP, None, VOC),
        P(REP, None, VOC),
        P(REP, VOC),
        P(REP, VOC),
        P(REP, VOC, None),
        P(REP, None),
    )
    return jax.shard_map(shards, mesh=fine, in_specs=placed, out_specs=P(REP, VOC), check_vma=False)
```

```python
import jax
import jax.numpy as jnp
from jax import lax
from jax.sharding import Mesh, PartitionSpec as P

outer_mu = 0.9
outer_lr = 0.7

REP = ("zlo", "core")
VOC = ("x", "y", "zhi")
SWAP = [(0, 1), (1, 0)]
RING = 4


def pick(a, i, axis):
    return lax.dynamic_index_in_dim(a, i, axis, False)


def shift(a, axis, by):
    n = lax.axis_size(axis)
    return lax.ppermute(a, axis, [(i, (i + by) % n) for i in range(n)])


def after(a, *deps):
    return lax.optimization_barrier((a,) + deps)[0]


def near(a, axis):
    return shift(a, axis, 1), shift(a, axis, -1)


def far(lower, upper, axis):
    block = jnp.where(lax.axis_index("core") == 0, lower, upper)
    up = [(i, (i + 1) % RING) for i in range(RING)]
    down = [(RING + j, RING + i) for i, j in up]
    return lax.ppermute(block, ("core", axis), up + down)


def cat(*a):
    return jnp.concatenate(a, 0)


def shards(codes, block_scales, outer_head, momentum, hidden, targets):
    zlo = lax.axis_index("zlo")
    core = lax.axis_index("core")
    x = lax.axis_index("x")
    y = lax.axis_index("y")
    zhi = lax.axis_index("zhi")
    replicas = 4
    rows, width = outer_head.shape
    tok = hidden.shape[1]
    f32, bf16 = jnp.float32, jnp.bfloat16

    blocks = block_scales.shape[1] // replicas
    per = rows // blocks
    c4 = codes.reshape(2, 2, rows, width)
    s4 = block_scales.reshape(2, 2, blocks, width)
    got_c = lax.ppermute(pick(c4, 1 - core, 1), "core", SWAP)
    got_s = lax.ppermute(pick(s4, 1 - core, 1), "core", SWAP)
    mine_c = pick(c4, core, 1)
    mine_s = pick(s4, core, 1)

    hid = hidden[0].reshape(tok, replicas, rows).transpose(1, 0, 2)
    hid = lax.all_to_all(hid, REP, 0, 0, tiled=True)

    def chip_sum(z):
        def term(c, s):
            c = pick(c, z, 0).astype(f32).reshape(blocks, per, width)
            return c * pick(s, z, 0).astype(f32)[:, None, :]
        return (term(mine_c, mine_s) + term(got_c, got_s)).reshape(rows, width)

    send = chip_sum(1 - zlo).astype(bf16)
    hid = after(hid, send)
    other = lax.ppermute(send, "zlo", SWAP)
    za, zb = near(hid, "zhi")
    a0, b0 = near(hid, "y")
    f0 = far(a0, b0, "y")
    za = after(za, a0, b0)
    zf = far(za, zb, "zhi")
    mid = cat(za, zb)
    a1, b1 = near(mid, "y")
    other = after(other, za, zb)
    pseudo = (chip_sum(zlo) + other.astype(f32)) * (1.0 / replicas)
    velocity = outer_mu * momentum + pseudo
    new = (outer_head.astype(f32) - outer_lr * (pseudo + outer_mu * velocity)).astype(bf16)
    xa, xb = near(new, "x")
    f1 = far(a1, b1, "y")
    a2, b2 = near(after(zf, a1, b1), "y")
    xf = far(xa, xb, "x")
    f2 = far(a2, b2, "y")

    def stack(own, lower, upper, ends):
        n = own.shape[0] // replicas
        buf = jnp.zeros((n, 4, replicas * tok, rows), bf16)
        for dy, blk in ((0, own), (-1, lower), (1, upper), (2, ends)):
            blk = blk.reshape(n, 1, replicas * tok, rows)
            buf = lax.dynamic_update_slice(buf, blk, (0, (y + dy) % 4, 0, 0))
        return buf.reshape(n * 4 * replicas * tok, rows)

    lhs1 = cat(stack(hid, a0, b0, f0), stack(mid, a1, b1, f1))
    lhs2 = stack(zf, a2, b2, f2)

    heads = [new, xa, xb, xf]
    away = (0, -1, 1, 2)

    want = lax.dynamic_slice_in_dim(targets[0], x * 16 * tok, 16 * tok, 0).reshape(4, 4, tok)
    want = want.transpose(1, 0, 2)
    want = lax.dynamic_slice_in_dim(cat(want, want), zhi, 4, 0)
    want = jnp.stack([want[d % 4] for d in away]).reshape(16, tok)
    place = y * 4 + zhi

    def reduce_part(units):
        part = cat(*[
            jnp.dot(lhs, heads[j], preferred_element_type=f32).reshape(-1, 2, 2, tok, width)
            for _, lhs, j in units
        ])
        both = lax.ppermute(pick(part, 1 - core, 2), "core", SWAP) + pick(part, core, 2)
        rest = lax.ppermute(pick(both, 1 - zlo, 1), "zlo", SWAP)
        logits = rest + pick(both, zlo, 1)
        at = 0
        for g, lhs, j in units:
            n = lhs.shape[0] // (replicas * tok)
            part = logits[at:at + n]
            at += n
            first = (((x + away[j]) % 4) * 16 + place) * width
            ids = lax.broadcasted_iota(jnp.int32, (1, 1, width), 2) + first
            top = jnp.max(part, axis=2)
            total = jnp.sum(jnp.exp(part - top[:, :, None]), axis=2)
            hit = jnp.sum(jnp.where(ids == want[g:g + n, :, None], part, 0.0), axis=2)
            stats[g, j] = jnp.stack([top, total, hit], axis=1)

    stats = {}
    reduce_part([(0, lhs1, 0)])
    reduce_part([(0, lhs1, 1), (0, lhs1, 2)])
    reduce_part([(0, lhs1, 3)] + [(12, lhs2, j) for j in range(4)])
    table = jnp.stack([cat(stats[0, j], stats[12, j]) for j in range(4)], axis=1)
    table = table.reshape(4, 4, 12 * tok)
    table = jnp.stack([table[away.index(d)] for d in (0, 1, 2, -1)])
    table = lax.dynamic_slice_in_dim(cat(table, table), (4 - zhi) % 4, 4, 0)
    table = lax.all_to_all(table.reshape(16, 12 * tok), ("zhi", "y"), 0, 0, tiled=True)
    table = table.reshape(64, 3, tok)
    top, total, hit = table[:, 0], table[:, 1], table[:, 2]
    high = jnp.max(top, axis=0)
    total = jnp.sum(total * jnp.exp(top - high), axis=0)
    loss = high + jnp.log(total) - jnp.sum(hit, axis=0)
    return loss[None, :]


def solution(mesh):
    fine = Mesh(mesh.devices.reshape(2, 2, 4, 4, 4), REP + VOC)
    placed = (
        P(REP, None, VOC),
        P(REP, None, VOC),
        P(REP, VOC),
        P(REP, VOC),
        P(REP, VOC, None),
        P(REP, None),
    )
    return jax.shard_map(shards, mesh=fine, in_specs=placed, out_specs=P(REP, VOC), check_vma=False)
```

```python
import jax
import jax.numpy as jnp
from jax import lax
from jax.sharding import Mesh, PartitionSpec as P

outer_mu = 0.9
outer_lr = 0.7

REP = ("zlo", "core")
VOC = ("x", "y", "zhi")
SWAP = [(0, 1), (1, 0)]
RING = 4


def pick(a, i, axis):
    return lax.dynamic_index_in_dim(a, i, axis, False)


def shift(a, axis, by):
    n = lax.axis_size(axis)
    return lax.ppermute(a, axis, [(i, (i + by) % n) for i in range(n)])


def after(a, *deps):
    return lax.optimization_barrier((a,) + deps)[0]


def near(a, axis):
    return shift(a, axis, 1), shift(a, axis, -1)


def far(lower, upper, axis):
    return onward(jnp.where(lax.axis_index("core") == 0, lower, upper), axis)


def onward(a, axis):
    up = [(i, (i + 1) % RING) for i in range(RING)]
    down = [(RING + j, RING + i) for i, j in up]
    return lax.ppermute(a, ("core", axis), up + down)


def cat(*a):
    return jnp.concatenate(a, 0)


def shards(codes, block_scales, outer_head, momentum, hidden, targets):
    zlo = lax.axis_index("zlo")
    core = lax.axis_index("core")
    x = lax.axis_index("x")
    y = lax.axis_index("y")
    zhi = lax.axis_index("zhi")
    replicas = 4
    rows, width = outer_head.shape
    tok = hidden.shape[1]
    f32, bf16 = jnp.float32, jnp.bfloat16

    blocks = block_scales.shape[1] // replicas
    per = rows // blocks
    c4 = codes.reshape(2, 2, rows, width)
    s4 = block_scales.reshape(2, 2, blocks, width)
    got_c = lax.ppermute(pick(c4, 1 - core, 1), "core", SWAP)
    got_s = lax.ppermute(pick(s4, 1 - core, 1), "core", SWAP)
    mine_c = pick(c4, core, 1)
    mine_s = pick(s4, core, 1)

    hid = hidden[0].reshape(tok, replicas, rows).transpose(1, 0, 2)
    hid = lax.all_to_all(hid, REP, 0, 0, tiled=True)

    def chip_sum(z):
        def term(c, s):
            c = pick(c, z, 0).astype(f32).reshape(blocks, per, width)
            return c * pick(s, z, 0).astype(f32)[:, None, :]
        return (term(mine_c, mine_s) + term(got_c, got_s)).reshape(rows, width)

    send = chip_sum(1 - zlo).astype(bf16)
    hid = after(hid, send)
    other = lax.ppermute(send, "zlo", SWAP)
    za, zb = near(hid, "zhi")
    a0, b0 = near(hid, "y")
    f0 = far(a0, b0, "y")
    za = after(za, a0, b0)
    mid = after(cat(za, zb), f0)
    a1, b1 = near(mid, "y")
    other = after(other, mid)
    zf = far(after(za, other), zb, "zhi")
    f1 = far(a1, b1, "y")
    pseudo = (chip_sum(zlo) + other.astype(f32)) * (1.0 / replicas)
    velocity = outer_mu * momentum + pseudo
    new = (outer_head.astype(f32) - outer_lr * (pseudo + outer_mu * velocity)).astype(bf16)
    xa, xb = near(new, "x")
    xf = far(xa, xb, "x")
    zfx = zf
    c1, c2 = near(zfx, "y")

    def put(buf, at, blk, dy):
        n = blk.shape[0] // replicas
        blk = blk.reshape(n, 1, replicas * tok, rows)
        return lax.dynamic_update_slice(buf, blk, (at, (y + 4 + dy) % 4, 0, 0))

    buf = jnp.zeros((3, 4, replicas * tok, rows), bf16)
    for at, own, lower, upper, ends in ((0, hid, a0, b0, f0), (1, mid, a1, b1, f1)):
        for dy, blk in ((0, own), (-1, lower), (1, upper), (2, ends)):
            buf = put(buf, at, blk, dy)
    lhs1 = buf.reshape(12 * replicas * tok, rows)

    away = (0, -1, 1, 2)

    want = lax.dynamic_slice_in_dim(targets[0], x * 16 * tok, 16 * tok, 0).reshape(4, 4, tok)
    want = want.transpose(1, 0, 2)
    want = lax.dynamic_slice_in_dim(cat(want, want), zhi, 4, 0)
    want = jnp.stack([want[d % 4] for d in away]).reshape(16, tok)
    place = y * 4 + zhi

    def partial(units, *deps):
        part = cat(*[
            jnp.dot(lhs, h, preferred_element_type=f32).reshape(-1, 2, 2, tok, width)
            for _, lhs, _, h in units
        ])
        half = pick(part, 1 - core, 2)
        if deps:
            half = after(half, *deps)
        both = lax.ppermute(half, "core", SWAP) + pick(part, core, 2)
        return both, pick(both, 1 - zlo, 1)

    stats = {}

    def finish(units, both, rest):
        logits = rest + pick(both, zlo, 1)
        at = 0
        for g, lhs, j, _ in units:
            n = lhs.shape[0] // (replicas * tok)
            part = logits[at:at + n]
            at += n
            first = (((x + away[j]) % 4) * 16 + place) * width
            ids = lax.broadcasted_iota(jnp.int32, (1, 1, width), 2) + first
            top = jnp.max(part, axis=2)
            total = jnp.sum(jnp.exp(part - top[:, :, None]), axis=2)
            hit = jnp.sum(jnp.where(ids == want[g:g + n, :, None], part, 0.0), axis=2)
            stats[g, j] = jnp.stack([top, total, hit], axis=1)

    u1 = [(0, lhs1, 0, new), (0, lhs1, 1, xa)]
    both1, send1 = partial(u1)
    rest1 = lax.ppermute(send1, "zlo", SWAP)
    u2 = [(0, lhs1, 2, after(xb, send1))]
    both2, send2 = partial(u2)
    rest2 = lax.ppermute(after(send2, rest1), "zlo", SWAP)
    c3 = far(c1, c2, "y")
    buf = jnp.zeros((1, 4, replicas * tok, rows), bf16)
    for dy, blk in ((0, zf), (-1, c1), (1, c2), (2, c3)):
        buf = put(buf, 0, blk, dy)
    lhs2 = buf.reshape(4 * replicas * tok, rows)
    xf = after(xf, rest1)
    u3 = [(0, lhs1, 3, xf)] + [(12, lhs2, j, h) for j, h in enumerate((new, xa, xb, xf))]
    both3, send3 = partial(u3, rest2)
    rest3 = lax.ppermute(after(send3, rest2), "zlo", SWAP)
    finish(u1, both1, rest1)
    finish(u2, both2, rest2)
    finish(u3, both3, rest3)

    table = jnp.stack([cat(stats[0, j], stats[12, j]) for j in range(4)], axis=1)
    table = table.reshape(4, 4, 12 * tok)
    table = jnp.stack([table[away.index(d)] for d in (0, 1, 2, -1)])
    table = lax.dynamic_slice_in_dim(cat(table, table), (4 - zhi) % 4, 4, 0)
    table = lax.all_to_all(table.reshape(16, 12 * tok), ("zhi", "y"), 0, 0, tiled=True)
    table = table.reshape(64, 3, tok)
    top, total, hit = table[:, 0], table[:, 1], table[:, 2]
    high = jnp.max(top, axis=0)
    total = jnp.sum(total * jnp.exp(top - high), axis=0)
    loss = high + jnp.log(total) - jnp.sum(hit, axis=0)
    return loss[None, :]


def solution(mesh):
    fine = Mesh(mesh.devices.reshape(2, 2, 4, 4, 4), REP + VOC)
    placed = (
        P(REP, None, VOC),
        P(REP, None, VOC),
        P(REP, VOC),
        P(REP, VOC),
        P(REP, VOC, None),
        P(REP, None),
    )
    return jax.shard_map(shards, mesh=fine, in_specs=placed, out_specs=P(REP, VOC), check_vma=False)
```

```python
import jax
import jax.numpy as jnp
from jax import lax
from jax.sharding import Mesh, PartitionSpec as P

outer_mu = 0.9
outer_lr = 0.7

REP = ("zlo", "core")
VOC = ("x", "y", "zhi")
SWAP = [(0, 1), (1, 0)]
RING = 4


def pick(a, i, axis):
    return lax.dynamic_index_in_dim(a, i, axis, False)


def shift(a, axis, by):
    n = lax.axis_size(axis)
    return lax.ppermute(a, axis, [(i, (i + by) % n) for i in range(n)])


def after(a, *deps):
    return lax.optimization_barrier((a,) + deps)[0]


def near(a, axis):
    return shift(a, axis, 1), shift(a, axis, -1)


def far(lower, upper, axis):
    return onward(jnp.where(lax.axis_index("core") == 0, lower, upper), axis)


def onward(a, axis):
    up = [(i, (i + 1) % RING) for i in range(RING)]
    down = [(RING + j, RING + i) for i, j in up]
    return lax.ppermute(a, ("core", axis), up + down)


def cat(*a):
    return jnp.concatenate(a, 0)


def shards(codes, block_scales, outer_head, momentum, hidden, targets):
    zlo = lax.axis_index("zlo")
    core = lax.axis_index("core")
    x = lax.axis_index("x")
    y = lax.axis_index("y")
    zhi = lax.axis_index("zhi")
    replicas = 4
    rows, width = outer_head.shape
    tok = hidden.shape[1]
    f32, bf16 = jnp.float32, jnp.bfloat16

    blocks = block_scales.shape[1] // replicas
    per = rows // blocks
    c4 = codes.reshape(2, 2, rows, width)
    s4 = block_scales.reshape(2, 2, blocks, width)
    got_c = lax.ppermute(pick(c4, 1 - core, 1), "core", SWAP)
    got_s = lax.ppermute(pick(s4, 1 - core, 1), "core", SWAP)
    mine_c = pick(c4, core, 1)
    mine_s = pick(s4, core, 1)

    hid = hidden[0].reshape(tok, replicas, rows).transpose(1, 0, 2)
    hid = lax.all_to_all(hid, REP, 0, 0, tiled=True)

    def chip_sum(z):
        def term(c, s):
            c = pick(c, z, 0).astype(f32).reshape(blocks, per, width)
            return c * pick(s, z, 0).astype(f32)[:, None, :]
        return (term(mine_c, mine_s) + term(got_c, got_s)).reshape(rows, width)

    send = chip_sum(1 - zlo).astype(bf16)
    hid = after(hid, send)
    other = lax.ppermute(send, "zlo", SWAP)
    za, zb = near(hid, "zhi")
    a0, b0 = near(hid, "y")
    f0 = far(a0, b0, "y")
    za = after(za, a0, b0)
    mid = after(cat(za, zb), f0)
    a1, b1 = near(mid, "y")
    other = after(other, mid)
    zf = far(after(za, other), zb, "zhi")
    f1 = far(a1, b1, "y")
    pseudo = (chip_sum(zlo) + other.astype(f32)) * (1.0 / replicas)
    velocity = outer_mu * momentum + pseudo
    new = (outer_head.astype(f32) - outer_lr * (pseudo + outer_mu * velocity)).astype(bf16)
    xa, xb = near(new, "x")
    xf = far(xa, xb, "x")
    zfx = zf
    c1, c2 = near(zfx, "y")

    def put(buf, at, blk, dy):
        n = blk.shape[0] // replicas
        blk = blk.reshape(n, 1, replicas * tok, rows)
        return lax.dynamic_update_slice(buf, blk, (at, (y + 4 + dy) % 4, 0, 0))

    buf = jnp.zeros((3, 4, replicas * tok, rows), bf16)
    for at, own, lower, upper, ends in ((0, hid, a0, b0, f0), (1, mid, a1, b1, f1)):
        for dy, blk in ((0, own), (-1, lower), (1, upper), (2, ends)):
            buf = put(buf, at, blk, dy)
    lhs1 = buf.reshape(12 * replicas * tok, rows)

    away = (0, -1, 1, 2)

    want = lax.dynamic_slice_in_dim(targets[0], x * 16 * tok, 16 * tok, 0).reshape(4, 4, tok)
    want = want.transpose(1, 0, 2)
    want = lax.dynamic_slice_in_dim(cat(want, want), zhi, 4, 0)
    want = jnp.stack([want[d % 4] for d in away]).reshape(16, tok)
    place = y * 4 + zhi

    def partial(units, *deps):
        part = cat(*[
            jnp.dot(lhs, h, preferred_element_type=f32).reshape(-1, 2, 2, tok, width)
            for _, lhs, _, h in units
        ])
        half = pick(part, 1 - core, 2)
        if deps:
            half = after(half, *deps)
        both = lax.ppermute(half, "core", SWAP) + pick(part, core, 2)
        return both, pick(both, 1 - zlo, 1)

    stats = {}

    def finish(units, both, rest):
        logits = rest + pick(both, zlo, 1)
        at = 0
        for g, lhs, j, _ in units:
            n = lhs.shape[0] // (replicas * tok)
            part = logits[at:at + n]
            at += n
            first = (((x + away[j]) % 4) * 16 + place) * width
            ids = lax.broadcasted_iota(jnp.int32, (1, 1, width), 2) + first
            top = jnp.max(part, axis=2)
            total = jnp.sum(jnp.exp(part - top[:, :, None]), axis=2)
            hit = jnp.sum(jnp.where(ids == want[g:g + n, :, None], part, 0.0), axis=2)
            stats[g, j] = jnp.stack([top, total, hit], axis=1)

    u1 = [(0, lhs1, 0, new), (0, lhs1, 1, xa)]
    both1, send1 = partial(u1)
    rest1 = lax.ppermute(send1, "zlo", SWAP)
    u2 = [(0, lhs1, 2, after(xb, send1))]
    both2, send2 = partial(u2)
    rest2 = lax.ppermute(after(send2, rest1), "zlo", SWAP)
    c3 = far(c1, c2, "y")
    buf = jnp.zeros((1, 4, replicas * tok, rows), bf16)
    for dy, blk in ((0, zf), (-1, c1), (1, c2), (2, c3)):
        buf = put(buf, 0, blk, dy)
    lhs2 = buf.reshape(4 * replicas * tok, rows)
    xf = after(xf, rest1)
    u3 = [(0, lhs1, 3, xf)] + [(12, lhs2, j, h) for j, h in enumerate((new, xa, xb, xf))]
    both3, send3 = partial(u3, rest2)
    rest3 = lax.ppermute(after(send3, rest2), "zlo", SWAP)
    finish(u1, both1, rest1)
    finish(u2, both2, rest2)
    finish(u3, both3, rest3)

    table = jnp.stack([cat(stats[0, j], stats[12, j]) for j in range(4)], axis=1)
    top = jnp.max(table[:, :, 0], axis=1)
    total = jnp.sum(table[:, :, 1] * jnp.exp(table[:, :, 0] - top[:, None]), axis=1)
    table = jnp.concatenate([top, total, jnp.sum(table[:, :, 2], axis=1)], axis=1).reshape(4, 4, 3 * tok)
    table = jnp.stack([table[away.index(d)] for d in (0, 1, 2, -1)])
    table = lax.dynamic_slice_in_dim(cat(table, table), (4 - zhi) % 4, 4, 0)
    table = lax.all_to_all(table.reshape(16, 3 * tok), ("zhi", "y"), 0, 0, tiled=True)
    table = table.reshape(16, 3, tok)
    top, total, hit = table[:, 0], table[:, 1], table[:, 2]
    high = jnp.max(top, axis=0)
    total = jnp.sum(total * jnp.exp(top - high), axis=0)
    loss = high + jnp.log(total) - jnp.sum(hit, axis=0)
    return loss[None, :]


def solution(mesh):
    fine = Mesh(mesh.devices.reshape(2, 2, 4, 4, 4), REP + VOC)
    placed = (
        P(REP, None, VOC),
        P(REP, None, VOC),
        P(REP, VOC),
        P(REP, VOC),
        P(REP, VOC, None),
        P(REP, None),
    )
    return jax.shard_map(shards, mesh=fine, in_specs=placed, out_specs=P(REP, VOC), check_vma=False)
```
